768 devices in a mesh: grp: 16 (over y, z_hi), sub: 48 (over x, z_lo, core).
Axes of the slice: x: 4, y: 8, z: 12 (z_hi: 2, z_lo: 6; z = z_hi * 6 + z_lo), core: 2. Of those that a mesh axis runs over, the one named last changes fastest.
Arguments:
- attn: bfloat16 [4096, 6144], P('grp', 'sub'), may hold values from -6 to 6
- grad_out: bfloat16 [4096, 12288], P('grp'), may hold values from -6 to 6
- w_values: bfloat16 [6144, 12288], P('sub', 'grp'), may hold values from -6 to 6
- w_scales: float32 [6144, 48], P('sub', 'grp'), may hold values from 0.00637888 to 0.02551552
Outputs:
- grad_attn: bfloat16 [4096, 6144], P('grp', 'sub')
- grad_w: bfloat16 [6144, 12288], P('sub', 'grp')
The draws below stay inside these ranges and needn't reach their ends.
All inputs are finite; a program needn't handle non-finite values. Where the reference program divides by a largest or mean magnitude, that divisor is 1e-20 or more.
Results may differ from the reference program's by a relative error of at most 0.0049.
Values may be sent and summed in bfloat16 or wider, within the bound.
A program may use at most 64 MiB of HBM per device.

```python
import math
import jax
import jax.numpy as jnp
from jax import lax

D = 12288
HD = 128
BLOCK = 256
TOK_G = 256
HEADS = 48
TOKENS = 4096
N_GRP = 16


def strengthened(values, own_key, source, target, shards_of, factor):
    def block_of(position):
        return (jnp.arange(values.shape[position]) // (values.shape[position] // shards_of)).reshape((-1,) + (1,) * (values.ndim - 1 - position))

    near = jax.random.permutation(own_key, shards_of)[block_of(target)]
    other_side = (block_of(target) + shards_of // 2) % shards_of
    return jnp.where((block_of(source) == near) | (block_of(source) == other_side), factor * values, values)


def shard_levels(stream_key, shape, pieces, smallest, top_value):
    gain, own = 1.0, jax.random.fold_in(stream_key, 6)
    for dim, blocks in pieces:
        draws = jnp.exp(jax.random.uniform(jax.random.fold_in(own, dim), (blocks,), jnp.float32, smallest / len(pieces), top_value / len(pieces)))
        gain = gain * jnp.repeat(draws, shape[dim] // blocks).reshape([-1 if axis == dim else 1 for axis in range(len(shape))])
    return gain


def centred(own_key, extent, width, bound, cuts=(), held_as=jnp.bfloat16):
    factor_of = shard_levels(own_key, extent, cuts, -0.22, 0.18) if cuts else 1.0
    array = jax.random.normal(own_key, extent, jnp.float32) * width * factor_of
    return jnp.minimum(jnp.maximum(array, -bound), bound).astype(held_as)


def gaussian_with(rng, extent, scale, reach, pieces, heavy, kind=jnp.bfloat16):
    entries = scale * jax.random.normal(rng, extent, jnp.float32)
    if pieces:
        entries = entries * shard_levels(rng, extent, pieces, -0.22, 0.18)
    return jnp.clip(strengthened(entries, jax.random.fold_in(rng, 3), *heavy), -reach, reach).astype(kind)


def setup_inputs(seed: int = 0) -> dict:
    streams_of = jax.random.split(jax.random.key(seed), 5)
    return {
        "attn": centred(streams_of[0], (TOKENS, HEADS * HD), 1.0, 6.0, ((0, 16), (1, 48))),
        "grad_out": gaussian_with(streams_of[1], (TOKENS, D), 1.0, 6.0, ((0, 16),), (0, 1, 16, 2.0)),
        "w_values": centred(streams_of[2], (HEADS * HD, D), 1.0, 6.0, ((0, 48), (1, 16))),
        "w_scales": jnp.clip(jnp.exp(math.log(0.02551552) - 1.3862944 * jax.random.uniform(streams_of[3], (HEADS * HD, D // BLOCK), jnp.float32) ** shard_levels(streams_of[3], (HEADS * HD, D // BLOCK), ((0, 48), (1, 16)), -0.2, 0.2)), 0.00637888, 0.02551552),
    }


def reference(attn, grad_out, w_values, w_scales):
    rows_w = HEADS * HD
    scale_full = jnp.repeat(w_scales, BLOCK, axis=1)
    weight = (w_values.astype(jnp.float32) * scale_full).astype(jnp.bfloat16)
    grad_attn = jnp.dot(grad_out, weight.T, preferred_element_type=jnp.float32).astype(jnp.bfloat16)
    summed = jnp.zeros((rows_w, D), jnp.float32)
    for group in range(N_GRP):
        tokens_a = attn[group * TOK_G:(group + 1) * TOK_G]
        tokens_d = grad_out[group * TOK_G:(group + 1) * TOK_G]
        part = jnp.dot(tokens_a.T, tokens_d, preferred_element_type=jnp.float32)
        blocks = part.reshape(rows_w, D // BLOCK, BLOCK)
        largest = (lax.optimization_barrier(jnp.max(jnp.abs(blocks), axis=2, keepdims=True)) + 1e-06).astype(jnp.bfloat16)
        largest = lax.optimization_barrier(largest).astype(jnp.float32)
        quant = (blocks / largest).astype(jnp.bfloat16)
        quant = lax.optimization_barrier(quant).astype(jnp.float32)
        summed = summed + (quant * largest).reshape(rows_w, D)
    total = jnp.sum(summed * summed)
    clip = jnp.minimum(1.0, 0.5 * jnp.sqrt(jnp.float32(rows_w * D)) / jnp.sqrt(total))
    return (grad_attn, (summed * clip).astype(jnp.bfloat16))
```

```python
import jax
import jax.numpy as jnp
from jax import lax
from jax.experimental import pallas as pl
from jax.experimental.pallas import tpu as pltpu
from jax.sharding import PartitionSpec as P

BLOCK = 256
NY, NZH, NX, NZL, NC = 8, 2, 4, 6, 2
NZ = NZH * NZL
MESH = pl.DeviceIdType.MESH
F32, BF16 = jnp.float32, jnp.bfloat16

UP = ((4, 0), (3, 1), (3, 0), (2, 1), (2, 0), (1, 1), (1, 0))
DOWN = ((4, 1), (3, 0), (3, 1), (2, 0), (2, 1), (1, 0), (1, 1))


def body(
    attn_ref, go_hbm, wv_ref, ws_ref, ga_ref, gw_ref,
    go, attn_t, w_own, w_got, rs_send, rs_got, own_sum, z_send, z_got, tile, tiles,
    go_sem, wz_sem, ag_sem, rs_sem, z_sem, ar_sem,
):
    grp, sub = lax.axis_index("grp"), lax.axis_index("sub")
    y, zh = grp // NZH, grp % NZH
    x, zl, core = sub // (NZL * NC), (sub // NC) % NZL, sub % NC
    z, xc = zh * NZL + zl, x * NC + core
    cols = wv_ref.shape[1]

    def along_y(d):
        return (((y + d) % NY) * NZH + zh, sub)

    def along_z(d):
        other = (z + d) % NZ
        return (y * NZH + other // NZL, (x * NZL + other % NZL) * NC + core)

    def along_xc(d):
        other = (xc + d) % (NX * NC)
        return (grp, ((other // NC) * NZL + zl) * NC + other % NC)

    sent = []

    def send(src, dst, sems, to):
        copy = pltpu.make_async_remote_copy(
            src_ref=src, dst_ref=dst, send_sem=sems[0], recv_sem=sems[1],
            device_id=to, device_id_type=MESH,
        )
        copy.start()
        sent.append(copy)
        return copy

    barrier = pltpu.get_barrier_semaphore()
    partners = [along_y(d) for d in range(1, NY)] + [along_z(d) for d in range(1, NZ)]
    partners += [along_xc(d) for d in range(1, NX * NC)]
    for to in partners:
        pl.semaphore_signal(barrier, inc=1, device_id=to, device_id_type=MESH)

    loads = {}
    for d in (4, 3, 5, 2, 6, 1, 7, 0):
        for h in (0, 1):
            chunk = ((y + d) % NY) * NZH + h
            loads[d, h] = pltpu.make_async_copy(
                go_hbm.at[:, pl.ds(pl.multiple_of(chunk * cols, cols), cols)],
                go.at[d, h],
                go_sem.at[d, h],
            )
            loads[d, h].start()

    scaled = [
        (wv_ref[:, j * BLOCK:(j + 1) * BLOCK].astype(F32) * ws_ref[:, j:j + 1]).astype(BF16)
        for j in range(cols // BLOCK)
    ]
    w_own[zh] = jnp.concatenate(scaled, axis=1)
    attn_t[...] = attn_ref[...].T

    pl.semaphore_wait(barrier, len(partners))
    opposite = along_z(NZL)
    w_z = send(w_own.at[zh], w_own.at[zh], (wz_sem.at[0], wz_sem.at[1]), opposite)

    def part(d, h):
        if (d, h) in loads:
            loads.pop((d, h)).wait()
        return jnp.dot(attn_t[...], go[d, h], preferred_element_type=F32)

    ways = ((0, 1, UP), (1, -1, DOWN))
    got = {}
    for i in range(7):
        for way, sign, items in ways:
            d, h = items[i]
            piece = part((sign * d) % NY, h)
            if (way, d + 1, h) in got:
                before = got[way, d + 1, h]
                before[0].wait_recv()
                piece = piece + rs_got[way, before[1]].astype(F32)
            rs_send[way, i] = piece.astype(BF16)
            copy = send(
                rs_send.at[way, i], rs_got.at[way, i],
                (rs_sem.at[0, way, i], rs_sem.at[1, way, i]), along_y(sign),
            )
            got[way, d, h] = (copy, i)

    def pass_on(src, way, sign, d, h):
        return send(
            src, w_got.at[way, d - 1, h],
            (ag_sem.at[0, way, d - 1, h], ag_sem.at[1, way, d - 1, h]), along_y(sign),
        )

    w_z.wait_recv()
    gathered = {}
    for h in (0, 1):
        for way, sign, _ in ways:
            gathered[way, 1, h] = pass_on(w_own.at[h], way, sign, 1, h)

    for h in (0, 1):
        own_sum[h] = part(0, h)
    for i in (5, 6):
        for way, _, items in ways:
            h = items[i][1]
            got[way, 1, h][0].wait_recv()
            own_sum[h] += rs_got[way, i].astype(F32)
    z_send[...] = own_sum[1 - zh].astype(BF16)
    to_opposite = send(z_send, z_got, (z_sem.at[0], z_sem.at[1]), opposite)

    def product(d, h, w):
        return lax.dot_general(go[d % NY, h], w, (((1,), (1,)), ((), ())), preferred_element_type=F32)

    total = product(0, 0, w_own[0]) + product(0, 1, w_own[1])

    def ring_step(d, total):
        arrived = []
        for h in (0, 1):
            for way, sign, _ in ways:
                if (way, d, h) not in gathered:
                    continue
                gathered[way, d, h].wait_recv()
                arrived.append((way, sign, h))
                if d < 3 or (d == 3 and h == way):
                    gathered[way, d + 1, h] = pass_on(w_got.at[way, d - 1, h], way, sign, d + 1, h)
        for way, sign, h in arrived:
            total = total + product(-sign * d, h, w_got[way, d - 1, h])
        return total

    def spread(stage, first, count, along):
        copies = []
        for d in range(1, count):
            slot = first + d - 1
            copies.append(
                send(tile.at[stage], tiles.at[slot], (ar_sem.at[0, slot], ar_sem.at[1, slot]), along(d))
            )
        return copies

    def collect(stage, first, copies):
        value = tile[stage]
        for d, copy in enumerate(copies):
            copy.wait_recv()
            value = value + tiles[first + d]
        return value

    total = ring_step(1, total)
    to_opposite.wait_recv()
    summed = own_sum[zh] + z_got[...].astype(F32)
    own_sum[zh] = summed
    squares = jnp.sum((summed * summed).reshape(-1, 8, cols), axis=0)
    tile[0] = sum(squares[:, j * 128:(j + 1) * 128] for j in range(cols // 128))
    copies = spread(0, 0, NY, along_y)
    total = ring_step(2, total)
    tile[1] = collect(0, 0, copies)
    copies = spread(1, NY - 1, NZ, along_z)
    total = ring_step(3, total)
    tile[2] = collect(1, NY - 1, copies)
    copies = spread(2, NY + NZ - 2, NX * NC, along_xc)
    total = ring_step(4, total)
    ga_ref[...] = total.astype(BF16)
    squares = jnp.sum(collect(2, NY + NZ - 2, copies), keepdims=True)
    count = NY * NZH * NX * NZL * NC * own_sum.shape[1] * cols
    clip = jnp.minimum(1.0, 0.5 * jnp.sqrt(jnp.full((1, 1), count, F32)) / jnp.sqrt(squares))
    gw_ref[...] = (own_sum[zh] * clip).astype(BF16)
    for copy in sent:
        copy.wait_send()


def on_device(attn, grad_out, w_values, w_scales):
    tokens, head = attn.shape
    rows, cols = w_values.shape
    vmem = pl.BlockSpec(memory_space=pltpu.VMEM)
    dma = pltpu.SemaphoreType.DMA
    n_tiles = NY + NZ + NX * NC - 3
    return pl.pallas_call(
        body,
        out_shape=(
            jax.ShapeDtypeStruct((tokens, head), BF16),
            jax.ShapeDtypeStruct((rows, cols), BF16),
        ),
        in_specs=[vmem, pl.BlockSpec(memory_space=pl.ANY), vmem, vmem],
        out_specs=(vmem, vmem),
        scratch_shapes=[
            pltpu.VMEM((NY, 2, tokens, cols), BF16),
            pltpu.VMEM((head, tokens), BF16),
            pltpu.VMEM((2, rows, cols), BF16),
            pltpu.VMEM((2, 4, 2, rows, cols), BF16),
            pltpu.VMEM((2, 7, rows, cols), BF16),
            pltpu.VMEM((2, 7, rows, cols), BF16),
            pltpu.VMEM((2, rows, cols), F32),
            pltpu.VMEM((rows, cols), BF16),
            pltpu.VMEM((rows, cols), BF16),
            pltpu.VMEM((3, 8, 128), F32),
            pltpu.VMEM((n_tiles, 8, 128), F32),
            dma((NY, 2)),
            dma((2,)),
            dma((2, 2, 4, 2)),
            dma((2, 2, 7)),
            dma((2,)),
            dma((2, n_tiles)),
        ],
        compiler_params=pltpu.CompilerParams(
            collective_id=0, has_side_effects=True, vmem_limit_bytes=48 * 2**20
        ),
        cost_estimate=pl.CostEstimate(
            flops=4 * tokens * head * 16 * cols, bytes_accessed=8 * 2**20, transcendentals=0
        ),
    )(attn, grad_out, w_values, w_scales)


def solution(mesh):
    placed = (P("grp", "sub"), P("grp", None), P("sub", "grp"), P("sub", "grp"))
    return jax.shard_map(
        on_device,
        mesh=mesh,
        in_specs=placed,
        out_specs=(P("grp", "sub"), P("sub", "grp")),
        check_vma=False,
    )
```

```python
import jax
import jax.numpy as jnp
from jax import lax
from jax.experimental import pallas as pl
from jax.experimental.pallas import tpu as pltpu
from jax.sharding import PartitionSpec as P

BLOCK = 256
NY, NZH, NX, NZL, NC = 8, 2, 4, 6, 2
NZ = NZH * NZL
MESH = pl.DeviceIdType.MESH
F32, BF16 = jnp.float32, jnp.bfloat16

UP = ((4, 1), (3, 1), (2, 1), (1, 1), (3, 0), (2, 0), (1, 0))
DOWN = ((3, 1), (2, 1), (1, 1), (4, 0), (3, 0), (2, 0), (1, 0))


def body(
    attn_ref, go_hbm, wv_ref, ws_ref, ga_ref, gw_ref,
    go, attn_t, w_own, w_got, rs_send, rs_got, own_part, own_sum, z_send, z_got, tile, tiles,
    go_sem, wz_sem, ag_sem, rs_sem, z_sem, ar_sem,
):
    grp, sub = lax.axis_index("grp"), lax.axis_index("sub")
    y, zh = grp // NZH, grp % NZH
    x, zl, core = sub // (NZL * NC), (sub // NC) % NZL, sub % NC
    z, xc = zh * NZL + zl, x * NC + core
    cols, half = wv_ref.shape[1], wv_ref.shape[0] // 2

    def along_y(d):
        return (((y + d) % NY) * NZH + zh, sub)

    def along_z(d):
        other = (z + d) % NZ
        return (y * NZH + other // NZL, (x * NZL + other % NZL) * NC + core)

    def along_xc(d):
        other = (xc + d) % (NX * NC)
        return (grp, ((other // NC) * NZL + zl) * NC + other % NC)

    sent = []

    def send(src, dst, sems, to):
        copy = pltpu.make_async_remote_copy(
            src_ref=src, dst_ref=dst, send_sem=sems[0], recv_sem=sems[1],
            device_id=to, device_id_type=MESH,
        )
        copy.start()
        sent.append(copy)
        return copy

    barrier = pltpu.get_barrier_semaphore()
    partners = [along_y(d) for d in range(1, NY)] + [along_z(d) for d in range(1, NZ)]
    partners += [along_xc(d) for d in range(1, NX * NC)]
    for to in partners:
        pl.semaphore_signal(barrier, inc=1, device_id=to, device_id_type=MESH)

    loads = {}
    for h in (1, 0):
        for d in (4, 3, 5, 2, 6, 1, 7, 0):
            chunk = ((y + d) % NY) * NZH + (zh if h == 0 else 1 - zh)
            loads[d, h] = pltpu.make_async_copy(
                go_hbm.at[:, pl.ds(pl.multiple_of(chunk * cols, cols), cols)],
                go.at[d, h],
                go_sem.at[d, h],
            )
            loads[d, h].start()

    scaled = [
        (wv_ref[:, j * BLOCK:(j + 1) * BLOCK].astype(F32) * ws_ref[:, j:j + 1]).astype(BF16)
        for j in range(cols // BLOCK)
    ]
    w_own[0] = jnp.concatenate(scaled, axis=1)
    attn_t[...] = attn_ref[...].T

    pl.semaphore_wait(barrier, len(partners))
    opposite = along_z(NZL)
    w_z = send(w_own.at[0], w_own.at[1], (wz_sem.at[0], wz_sem.at[1]), opposite)

    def part(d, h):
        if (d, h) in loads:
            loads.pop((d, h)).wait()
        return jnp.dot(attn_t[...], go[d, h], preferred_element_type=F32)

    ways = ((0, 1, UP), (1, -1, DOWN))
    got = {}

    def reduce_step(i):
        for way, sign, items in ways:
            d, h = items[i]
            own_part[way] = part((sign * d) % NY, h)
        for r in (0, 1):
            for way, sign, items in ways:
                d, h = items[i]
                piece = own_part[way, pl.ds(r * half, half)]
                if (way, d + 1, h, r) in got:
                    before, place = got[way, d + 1, h, r]
                    before.wait_recv()
                    piece = piece + rs_got[way, place].astype(F32)
                k = 2 * i + r
                rs_send[way, k] = piece.astype(BF16)
                copy = send(
                    rs_send.at[way, k], rs_got.at[way, k],
                    (rs_sem.at[0, way, k], rs_sem.at[1, way, k]), along_y(sign),
                )
                got[way, d, h, r] = (copy, k)

    def reduce_end(h):
        own_sum[h] = part(0, h)
        for r in (0, 1):
            for way, _, _ in ways:
                copy, k = got[way, 1, h, r]
                copy.wait_recv()
                own_sum[h, pl.ds(r * half, half)] += rs_got[way, k].astype(F32)

    for i in range(5):
        reduce_step(i)
    reduce_end(1)
    z_send[...] = own_sum[1].astype(BF16)
    to_opposite = send(z_send, z_got, (z_sem.at[0], z_sem.at[1]), opposite)
    for i in (5, 6):
        reduce_step(i)

    def pass_on(src, way, sign, d, h):
        return send(
            src, w_got.at[way, d - 1, h],
            (ag_sem.at[0, way, d - 1, h], ag_sem.at[1, way, d - 1, h]), along_y(sign),
        )

    w_z.wait_recv()
    gathered = {}
    for h in (0, 1):
        for way, sign, _ in ways:
            gathered[way, 1, h] = pass_on(w_own.at[h], way, sign, 1, h)

    reduce_end(0)

    def product(d, h, w):
        return lax.dot_general(go[d % NY, h], w, (((1,), (1,)), ((), ())), preferred_element_type=F32)

    total = product(0, 0, w_own[0]) + product(0, 1, w_own[1])

    def ring_step(d, h, total):
        arrived = []
        for way, sign, _ in ways:
            if (way, d, h) not in gathered:
                continue
            gathered[way, d, h].wait_recv()
            arrived.append((way, sign))
            if d < 3 or (d == 3 and h == way):
                gathered[way, d + 1, h] = pass_on(w_got.at[way, d - 1, h], way, sign, d + 1, h)
        for way, sign in arrived:
            total = total + product(-sign * d, h, w_got[way, d - 1, h])
        return total

    def spread(stage, first, count, along):
        copies = []
        for d in range(1, count):
            slot = first + d - 1
            copies.append(
                send(tile.at[stage], tiles.at[slot], (ar_sem.at[0, slot], ar_sem.at[1, slot]), along(d))
            )
        return copies

    def collect(stage, first, copies):
        value = tile[stage]
        for d, copy in enumerate(copies):
            copy.wait_recv()
            value = value + tiles[first + d]
        return value

    total = ring_step(1, 0, total)
    to_opposite.wait_recv()
    summed = own_sum[0] + z_got[...].astype(F32)
    own_sum[0] = summed
    squares = jnp.sum((summed * summed).reshape(-1, 8, cols), axis=0)
    tile[0] = sum(squares[:, j * 128:(j + 1) * 128] for j in range(cols // 128))
    copies = spread(0, 0, NX * NC, along_xc)
    total = ring_step(1, 1, total)
    tile[1] = collect(0, 0, copies)
    copies = spread(1, NX * NC - 1, NZ, along_z)
    total = ring_step(2, 0, total)
    total = ring_step(2, 1, total)
    tile[2] = collect(1, NX * NC - 1, copies)
    copies = spread(2, NX * NC + NZ - 2, NY, along_y)
    total = ring_step(3, 0, total)
    total = ring_step(3, 1, total)
    squares = jnp.sum(collect(2, NX * NC + NZ - 2, copies), keepdims=True)
    count = NY * NZH * NX * NZL * NC * own_sum.shape[1] * cols
    clip = jnp.minimum(1.0, 0.5 * jnp.sqrt(jnp.full((1, 1), count, F32)) / jnp.sqrt(squares))
    gw_ref[...] = (own_sum[0] * clip).astype(BF16)
    total = ring_step(4, 0, total)
    total = ring_step(4, 1, total)
    ga_ref[...] = total.astype(BF16)
    for copy in sent:
        copy.wait_send()


def on_device(attn, grad_out, w_values, w_scales):
    tokens, head = attn.shape
    rows, cols = w_values.shape
    vmem = pl.BlockSpec(memory_space=pltpu.VMEM)
    dma = pltpu.SemaphoreType.DMA
    n_tiles = NY + NZ + NX * NC - 3
    return pl.pallas_call(
        body,
        out_shape=(
            jax.ShapeDtypeStruct((tokens, head), BF16),
            jax.ShapeDtypeStruct((rows, cols), BF16),
        ),
        in_specs=[vmem, pl.BlockSpec(memory_space=pl.ANY), vmem, vmem],
        out_specs=(vmem, vmem),
        scratch_shapes=[
            pltpu.VMEM((NY, 2, tokens, cols), BF16),
            pltpu.VMEM((head, tokens), BF16),
            pltpu.VMEM((2, rows, cols), BF16),
            pltpu.VMEM((2, 4, 2, rows, cols), BF16),
            pltpu.VMEM((2, 14, rows // 2, cols), BF16),
            pltpu.VMEM((2, 14, rows // 2, cols), BF16),
            pltpu.VMEM((2, rows, cols), F32),
            pltpu.VMEM((2, rows, cols), F32),
            pltpu.VMEM((rows, cols), BF16),
            pltpu.VMEM((rows, cols), BF16),
            pltpu.VMEM((3, 8, 128), F32),
            pltpu.VMEM((n_tiles, 8, 128), F32),
            dma((NY, 2)),
            dma((2,)),
            dma((2, 2, 4, 2)),
            dma((2, 2, 14)),
            dma((2,)),
            dma((2, n_tiles)),
        ],
        compiler_params=pltpu.CompilerParams(
            collective_id=0, has_side_effects=True, vmem_limit_bytes=48 * 2**20
        ),
        cost_estimate=pl.CostEstimate(
            flops=4 * tokens * head * 16 * cols, bytes_accessed=8 * 2**20, transcendentals=0
        ),
    )(attn, grad_out, w_values, w_scales)


def solution(mesh):
    placed = (P("grp", "sub"), P("grp", None), P("sub", "grp"), P("sub", "grp"))
    return jax.shard_map(
        on_device,
        mesh=mesh,
        in_specs=placed,
        out_specs=(P("grp", "sub"), P("sub", "grp")),
        check_vma=False,
    )
```

```python
import jax
import jax.numpy as jnp
from jax import lax
from jax.experimental import pallas as pl
from jax.experimental.pallas import tpu as pltpu
from jax.sharding import PartitionSpec as P

BLOCK = 256
NY, NZH, NX, NZL, NC = 8, 2, 4, 6, 2
NZ = NZH * NZL
MESH = pl.DeviceIdType.MESH
F32, BF16 = jnp.float32, jnp.bfloat16

UP = ((4, 1), (3, 1), (2, 1), (1, 1), (3, 0), (2, 0), (1, 0))
DOWN = ((3, 1), (2, 1), (1, 1), (4, 0), (3, 0), (2, 0), (1, 0))


def body(
    attn_hbm, go_hbm, wv_hbm, ws_hbm, ga_ref, gw_ref,
    attn_ref, wv_ref, ws_ref, go, attn_t, w_own, w_got, rs_send, rs_got, own_part, own_sum, z_send, z_got, tile, tiles,
    in_sem, go_sem, wz_sem, ag_sem, rs_sem, z_sem, ar_sem,
):
    grp, sub = lax.axis_index("grp"), lax.axis_index("sub")
    y, zh = grp // NZH, grp % NZH
    x, zl, core = sub // (NZL * NC), (sub // NC) % NZL, sub % NC
    z, xc = zh * NZL + zl, x * NC + core
    cols, half = wv_ref.shape[1], wv_ref.shape[0] // 2

    def along_y(d):
        return (((y + d) % NY) * NZH + zh, sub)

    def along_z(d):
        other = (z + d) % NZ
        return (y * NZH + other // NZL, (x * NZL + other % NZL) * NC + core)

    def along_xc(d):
        other = (xc + d) % (NX * NC)
        return (grp, ((other // NC) * NZL + zl) * NC + other % NC)

    sent = []

    def send(src, dst, sems, to):
        copy = pltpu.make_async_remote_copy(
            src_ref=src, dst_ref=dst, send_sem=sems[0], recv_sem=sems[1],
            device_id=to, device_id_type=MESH,
        )
        copy.start()
        sent.append(copy)
        return copy

    inputs = [
        pltpu.make_async_copy(src, dst, in_sem.at[i])
        for i, (src, dst) in enumerate(((attn_hbm, attn_ref), (wv_hbm, wv_ref), (ws_hbm, ws_ref)))
    ]
    for copy in inputs:
        copy.start()
    loads = {}
    for h in (1, 0):
        for d in (4, 5, 3, 6, 2, 7, 1, 0):
            chunk = ((y + d) % NY) * NZH + (zh if h == 0 else 1 - zh)
            loads[d, h] = pltpu.make_async_copy(
                go_hbm.at[:, pl.ds(pl.multiple_of(chunk * cols, cols), cols)],
                go.at[d, h],
                go_sem.at[d, h],
            )
            loads[d, h].start()

    barrier = pltpu.get_barrier_semaphore()
    partners = [along_y(d) for d in (1, 7, 2, 6, 3, 5, 4)] + [along_z(d) for d in range(1, NZ)]
    partners += [along_xc(d) for d in range(1, NX * NC)]
    for to in partners:
        pl.semaphore_signal(barrier, inc=1, device_id=to, device_id_type=MESH)

    inputs[0].wait()
    attn_t[...] = attn_ref[...].T
    pl.semaphore_wait(barrier, len(partners))
    opposite = along_z(NZL)

    def part(d, h):
        if (d, h) in loads:
            loads.pop((d, h)).wait()
        return jnp.dot(attn_t[...], go[d, h], preferred_element_type=F32)

    ways = ((0, 1, UP), (1, -1, DOWN))
    got = {}

    def reduce_step(i):
        for way, sign, items in ways:
            d, h = items[i]
            own_part[way] = part((sign * d) % NY, h)
        for r in (0, 1):
            for way, sign, items in ways:
                d, h = items[i]
                piece = own_part[way, pl.ds(r * half, half)]
                if (way, d + 1, h, r) in got:
                    before, place = got[way, d + 1, h, r]
                    before.wait_recv()
                    piece = piece + rs_got[way, place].astype(F32)
                k = 2 * i + r
                rs_send[way, k] = piece.astype(BF16)
                copy = send(
                    rs_send.at[way, k], rs_got.at[way, k],
                    (rs_sem.at[0, way, k], rs_sem.at[1, way, k]), along_y(sign),
                )
                got[way, d, h, r] = (copy, k)

    def reduce_end(h):
        own_sum[h] = part(0, h)
        for r in (0, 1):
            for way, _, _ in ways:
                copy, k = got[way, 1, h, r]
                copy.wait_recv()
                own_sum[h, pl.ds(r * half, half)] += rs_got[way, k].astype(F32)

    def pass_on(src, way, sign, d, h):
        return send(
            src, w_got.at[way, d - 1, h],
            (ag_sem.at[0, way, d - 1, h], ag_sem.at[1, way, d - 1, h]), along_y(sign),
        )

    gathered = {}

    def first_pass(h):
        for way, sign, _ in ways:
            gathered[way, 1, h] = pass_on(w_own.at[h], way, sign, 1, h)

    reduce_step(0)
    for copy in inputs[1:]:
        copy.wait()
    for j in range(cols // BLOCK):
        scale = jnp.broadcast_to(ws_ref[j:j + 1, :], (ws_ref.shape[1], ws_ref.shape[1])).T
        for k in range(j * BLOCK, (j + 1) * BLOCK, scale.shape[1]):
            piece = slice(k, k + scale.shape[1])
            w_own[0, :, piece] = (wv_ref[:, piece].astype(F32) * scale).astype(BF16)
    w_z = send(w_own.at[0], w_own.at[1], (wz_sem.at[0], wz_sem.at[1]), opposite)
    for i in (1, 2, 3, 4):
        reduce_step(i)
    first_pass(0)
    reduce_end(1)
    z_send[...] = own_sum[1].astype(BF16)
    to_opposite = send(z_send, z_got, (z_sem.at[0], z_sem.at[1]), opposite)
    for i in (5, 6):
        reduce_step(i)

    w_z.wait_recv()
    first_pass(1)
    reduce_end(0)

    def product(d, h, w):
        return lax.dot_general(go[d % NY, h], w, (((1,), (1,)), ((), ())), preferred_element_type=F32)

    total = product(0, 0, w_own[0]) + product(0, 1, w_own[1])

    def ring_step(d, h, total):
        arrived = []
        for way, sign, _ in ways:
            if (way, d, h) not in gathered:
                continue
            gathered[way, d, h].wait_recv()
            arrived.append((way, sign))
            if d < 3 or (d == 3 and h == way):
                gathered[way, d + 1, h] = pass_on(w_got.at[way, d - 1, h], way, sign, d + 1, h)
        for way, sign in arrived:
            total = total + product(-sign * d, h, w_got[way, d - 1, h])
        return total

    def spread(stage, first, count, along):
        copies = []
        for d in range(1, count):
            slot = first + d - 1
            copies.append(
                send(tile.at[stage], tiles.at[slot], (ar_sem.at[0, slot], ar_sem.at[1, slot]), along(d))
            )
        return copies

    def collect(stage, first, copies):
        value = tile[stage]
        for d, copy in enumerate(copies):
            copy.wait_recv()
            value = value + tiles[first + d]
        return value

    total = ring_step(1, 0, total)
    to_opposite.wait_recv()
    summed = own_sum[0] + z_got[...].astype(F32)
    own_sum[0] = summed
    squares = jnp.sum((summed * summed).reshape(-1, 8, cols), axis=0)
    tile[0] = sum(squares[:, j * 128:(j + 1) * 128] for j in range(cols // 128))
    copies = spread(0, 0, NX * NC, along_xc)
    total = ring_step(1, 1, total)
    tile[1] = collect(0, 0, copies)
    copies = spread(1, NX * NC - 1, NZ, along_z)
    total = ring_step(2, 0, total)
    total = ring_step(2, 1, total)
    tile[2] = collect(1, NX * NC - 1, copies)
    copies = spread(2, NX * NC + NZ - 2, NY, along_y)
    total = ring_step(3, 0, total)
    total = ring_step(3, 1, total)
    squares = jnp.sum(collect(2, NX * NC + NZ - 2, copies), keepdims=True)
    count = NY * NZH * NX * NZL * NC * own_sum.shape[1] * cols
    clip = jnp.minimum(1.0, 0.5 * jnp.sqrt(jnp.full((1, 1), count, F32)) / jnp.sqrt(squares))
    gw_ref[...] = (own_sum[0] * clip).astype(BF16)
    total = ring_step(4, 0, total)
    total = ring_step(4, 1, total)
    ga_ref[...] = total.astype(BF16)
    for copy in sent:
        copy.wait_send()


def on_device(attn, grad_out, w_values, w_scales):
    tokens, head = attn.shape
    rows, cols = w_values.shape
    vmem = pl.BlockSpec(memory_space=pltpu.VMEM)
    dma = pltpu.SemaphoreType.DMA
    n_tiles = NY + NZ + NX * NC - 3
    return pl.pallas_call(
        body,
        out_shape=(
            jax.ShapeDtypeStruct((tokens, head), BF16),
            jax.ShapeDtypeStruct((rows, cols), BF16),
        ),
        in_specs=[pl.BlockSpec(memory_space=pltpu.HBM)] * 4,
        out_specs=(vmem, vmem),
        scratch_shapes=[
            pltpu.VMEM((tokens, head), BF16),
            pltpu.VMEM((rows, cols), BF16),
            pltpu.VMEM((cols // BLOCK, rows), F32),
            pltpu.VMEM((NY, 2, tokens, cols), BF16),
            pltpu.VMEM((head, tokens), BF16),
            pltpu.VMEM((2, rows, cols), BF16),
            pltpu.VMEM((2, 4, 2, rows, cols), BF16),
            pltpu.VMEM((2, 14, rows // 2, cols), BF16),
            pltpu.VMEM((2, 14, rows // 2, cols), BF16),
            pltpu.VMEM((2, rows, cols), F32),
            pltpu.VMEM((2, rows, cols), F32),
            pltpu.VMEM((rows, cols), BF16),
            pltpu.VMEM((rows, cols), BF16),
            pltpu.VMEM((3, 8, 128), F32),
            pltpu.VMEM((n_tiles, 8, 128), F32),
            dma((3,)),
            dma((NY, 2)),
            dma((2,)),
            dma((2, 2, 4, 2)),
            dma((2, 2, 14)),
            dma((2,)),
            dma((2, n_tiles)),
        ],
        compiler_params=pltpu.CompilerParams(
            collective_id=0, has_side_effects=True, vmem_limit_bytes=40 * 2**20
        ),
        cost_estimate=pl.CostEstimate(
            flops=4 * tokens * head * 16 * cols, bytes_accessed=8 * 2**20, transcendentals=0
        ),
    )(*(pltpu.with_memory_space_constraint(a, pltpu.HBM) for a in (attn, grad_out, w_values, w_scales.T)))


def solution(mesh):
    placed = (P("grp", "sub"), P("grp", None), P("sub", "grp"), P("sub", "grp"))
    return jax.shard_map(
        on_device,
        mesh=mesh,
        in_specs=placed,
        out_specs=(P("grp", "sub"), P("sub", "grp")),
        check_vma=False,
    )
```

```python
import jax
import jax.numpy as jnp
from jax import lax
from jax.experimental import pallas as pl
from jax.experimental.pallas import tpu as pltpu
from jax.sharding import PartitionSpec as P

BLOCK = 256
NY, NZH, NX, NZL, NC = 8, 2, 4, 6, 2
NZ = NZH * NZL
MESH = pl.DeviceIdType.MESH
F32, BF16 = jnp.float32, jnp.bfloat16

UP = ((4, 1), (3, 1), (2, 1), (1, 1), (3, 0), (2, 0), (1, 0))
DOWN = ((3, 1), (2, 1), (1, 1), (4, 0), (3, 0), (2, 0), (1, 0))


def body(
    attn_hbm, go_hbm, wv_hbm, ws_hbm, ga_ref, gw_ref,
    attn_ref, wv_ref, ws_ref, go, attn_t, w_own, w_got, rs_send, rs_got, own_part, own_sum, z_send, z_got, tile, tiles,
    in_sem, go_sem, wz_sem, ag_sem, rs_sem, z_sem, ar_sem,
):
    grp, sub = lax.axis_index("grp"), lax.axis_index("sub")
    y, zh = grp // NZH, grp % NZH
    x, zl, core = sub // (NZL * NC), (sub // NC) % NZL, sub % NC
    z, xc = zh * NZL + zl, x * NC + core
    cols, half, small = wv_ref.shape[1], wv_ref.shape[0] // 2, wv_ref.shape[0] // 4

    def along_y(d):
        return (((y + d) % NY) * NZH + zh, sub)

    def along_z(d):
        other = (z + d) % NZ
        return (y * NZH + other // NZL, (x * NZL + other % NZL) * NC + core)

    def along_xc(d):
        other = (xc + d) % (NX * NC)
        return (grp, ((other // NC) * NZL + zl) * NC + other % NC)

    sent = []

    def send(src, dst, sems, to):
        copy = pltpu.make_async_remote_copy(
            src_ref=src, dst_ref=dst, send_sem=sems[0], recv_sem=sems[1],
            device_id=to, device_id_type=MESH,
        )
        copy.start()
        sent.append(copy)
        return copy

    inputs = [
        pltpu.make_async_copy(src, dst, in_sem.at[i])
        for i, (src, dst) in enumerate(((attn_hbm, attn_ref), (wv_hbm, wv_ref), (ws_hbm, ws_ref)))
    ]
    for copy in inputs:
        copy.start()
    loads = {}
    for h in (1, 0):
        for d in (4, 5, 3, 6, 2, 7, 1, 0):
            chunk = ((y + d) % NY) * NZH + (zh if h == 0 else 1 - zh)
            loads[d, h] = pltpu.make_async_copy(
                go_hbm.at[:, pl.ds(pl.multiple_of(chunk * cols, cols), cols)],
                go.at[d, h],
                go_sem.at[d, h],
            )
            loads[d, h].start()

    barrier = pltpu.get_barrier_semaphore()
    partners = [along_y(d) for d in (1, 7, 2, 6, 3, 5, 4)] + [along_z(d) for d in range(1, NZ)]
    partners += [along_xc(d) for d in range(1, NX * NC)]
    for to in partners:
        pl.semaphore_signal(barrier, inc=1, device_id=to, device_id_type=MESH)

    inputs[0].wait()
    attn_t[...] = attn_ref[...].T
    pl.semaphore_wait(barrier, len(partners))
    opposite = along_z(NZL)

    def part(d, h):
        if (d, h) in loads:
            loads.pop((d, h)).wait()
        return jnp.dot(attn_t[...], go[d, h], preferred_element_type=F32)

    ways = ((0, 1, UP), (1, -1, DOWN))
    got = {}

    def reduce_step(i):
        for way, sign, items in ways:
            d, h = items[i]
            own_part[way] = part((sign * d) % NY, h)
        for r in range(4):
            for way, sign, items in ways:
                d, h = items[i]
                piece = own_part[way, pl.ds(r * small, small)]
                if (way, d + 1, h, r) in got:
                    before, place = got[way, d + 1, h, r]
                    before.wait_recv()
                    piece = piece + rs_got[way, place].astype(F32)
                k = 4 * i + r
                rs_send[way, k] = piece.astype(BF16)
                copy = send(
                    rs_send.at[way, k], rs_got.at[way, k],
                    (rs_sem.at[0, way, k], rs_sem.at[1, way, k]), along_y(sign),
                )
                got[way, d, h, r] = (copy, k)

    def reduce_end(h):
        own_sum[h] = part(0, h)
        for r in range(4):
            for way, _, _ in ways:
                copy, k = got[way, 1, h, r]
                copy.wait_recv()
                own_sum[h, pl.ds(r * small, small)] += rs_got[way, k].astype(F32)

    def pass_on(src, way, sign, d, h, q):
        return send(
            src, w_got.at[way, d - 1, h, pl.ds(q * half, half)],
            (ag_sem.at[0, way, d - 1, h, q], ag_sem.at[1, way, d - 1, h, q]), along_y(sign),
        )

    gathered = {}

    def first_pass(h):
        for way, sign, _ in ways:
            for q in (0, 1):
                gathered[way, 1, h, q] = pass_on(w_own.at[h, pl.ds(q * half, half)], way, sign, 1, h, q)

    reduce_step(0)
    for copy in inputs[1:]:
        copy.wait()
    for j in range(cols // BLOCK):
        scale = jnp.broadcast_to(ws_ref[j:j + 1, :], (ws_ref.shape[1], ws_ref.shape[1])).T
        for k in range(j * BLOCK, (j + 1) * BLOCK, scale.shape[1]):
            piece = slice(k, k + scale.shape[1])
            w_own[0, :, piece] = (wv_ref[:, piece].astype(F32) * scale).astype(BF16)
    w_z = send(w_own.at[0], w_own.at[1], (wz_sem.at[0], wz_sem.at[1]), opposite)
    for i in (1, 2, 3, 4):
        reduce_step(i)
    first_pass(0)
    reduce_end(1)
    z_send[...] = own_sum[1].astype(BF16)
    to_opposite = send(z_send, z_got, (z_sem.at[0], z_sem.at[1]), opposite)
    for i in (5, 6):
        reduce_step(i)

    w_z.wait_recv()
    first_pass(1)
    reduce_end(0)

    def product(d, h, w):
        return lax.dot_general(go[d % NY, h], w, (((1,), (1,)), ((), ())), preferred_element_type=F32)

    total = product(0, 0, w_own[0]) + product(0, 1, w_own[1])

    def ring_step(d, h, total):
        arrived = []
        for q in (0, 1):
            for way, sign, _ in ways:
                if (way, d, h, q) not in gathered:
                    continue
                gathered[way, d, h, q].wait_recv()
                if q:
                    arrived.append((way, sign))
                if d < 3 or (d == 3 and h == way):
                    src = w_got.at[way, d - 1, h, pl.ds(q * half, half)]
                    gathered[way, d + 1, h, q] = pass_on(src, way, sign, d + 1, h, q)
        for way, sign in arrived:
            total = total + product(-sign * d, h, w_got[way, d - 1, h])
        return total

    def spread(stage, first, count, along):
        copies = []
        for d in range(1, count):
            slot = first + d - 1
            copies.append(
                send(tile.at[stage], tiles.at[slot], (ar_sem.at[0, slot], ar_sem.at[1, slot]), along(d))
            )
        return copies

    def collect(stage, first, copies):
        value = tile[stage]
        for d, copy in enumerate(copies):
            copy.wait_recv()
            value = value + tiles[first + d]
        return value

    total = ring_step(1, 0, total)
    to_opposite.wait_recv()
    summed = own_sum[0] + z_got[...].astype(F32)
    own_sum[0] = summed
    squares = jnp.sum((summed * summed).reshape(-1, 8, cols), axis=0)
    tile[0] = sum(squares[:, j * 128:(j + 1) * 128] for j in range(cols // 128))
    copies = spread(0, 0, NX * NC, along_xc)
    total = ring_step(1, 1, total)
    tile[1] = collect(0, 0, copies)
    copies = spread(1, NX * NC - 1, NZ, along_z)
    total = ring_step(2, 0, total)
    total = ring_step(2, 1, total)
    tile[2] = collect(1, NX * NC - 1, copies)
    copies = spread(2, NX * NC + NZ - 2, NY, along_y)
    total = ring_step(3, 0, total)
    total = ring_step(3, 1, total)
    squares = jnp.sum(collect(2, NX * NC + NZ - 2, copies), keepdims=True)
    count = NY * NZH * NX * NZL * NC * own_sum.shape[1] * cols
    clip = jnp.minimum(1.0, 0.5 * jnp.sqrt(jnp.full((1, 1), count, F32)) / jnp.sqrt(squares))
    gw_ref[...] = (own_sum[0] * clip).astype(BF16)
    total = ring_step(4, 0, total)
    total = ring_step(4, 1, total)
    ga_ref[...] = total.astype(BF16)
    for copy in sent:
        copy.wait_send()


def on_device(attn, grad_out, w_values, w_scales):
    tokens, head = attn.shape
    rows, cols = w_values.shape
    vmem = pl.BlockSpec(memory_space=pltpu.VMEM)
    dma = pltpu.SemaphoreType.DMA
    n_tiles = NY + NZ + NX * NC - 3
    return pl.pallas_call(
        body,
        out_shape=(
            jax.ShapeDtypeStruct((tokens, head), BF16),
            jax.ShapeDtypeStruct((rows, cols), BF16),
        ),
        in_specs=[pl.BlockSpec(memory_space=pltpu.HBM)] * 4,
        out_specs=(vmem, vmem),
        scratch_shapes=[
            pltpu.VMEM((tokens, head), BF16),
            pltpu.VMEM((rows, cols), BF16),
            pltpu.VMEM((cols // BLOCK, rows), F32),
            pltpu.VMEM((NY, 2, tokens, cols), BF16),
            pltpu.VMEM((head, tokens), BF16),
            pltpu.VMEM((2, rows, cols), BF16),
            pltpu.VMEM((2, 4, 2, rows, cols), BF16),
            pltpu.VMEM((2, 28, rows // 4, cols), BF16),
            pltpu.VMEM((2, 28, rows // 4, cols), BF16),
            pltpu.VMEM((2, rows, cols), F32),
            pltpu.VMEM((2, rows, cols), F32),
            pltpu.VMEM((rows, cols), BF16),
            pltpu.VMEM((rows, cols), BF16),
            pltpu.VMEM((3, 8, 128), F32),
            pltpu.VMEM((n_tiles, 8, 128), F32),
            dma((3,)),
            dma((NY, 2)),
            dma((2,)),
            dma((2, 2, 4, 2, 2)),
            dma((2, 2, 28)),
            dma((2,)),
            dma((2, n_tiles)),
        ],
        compiler_params=pltpu.CompilerParams(
            collective_id=0, has_side_effects=True, vmem_limit_bytes=40 * 2**20
        ),
        cost_estimate=pl.CostEstimate(
            flops=4 * tokens * head * 16 * cols, bytes_accessed=8 * 2**20, transcendentals=0
        ),
    )(*(pltpu.with_memory_space_constraint(a, pltpu.HBM) for a in (attn, grad_out, w_values, w_scales.T)))


def solution(mesh):
    placed = (P("grp", "sub"), P("grp", None), P("sub", "grp"), P("sub", "grp"))
    return jax.shard_map(
        on_device,
        mesh=mesh,
        in_specs=placed,
        out_specs=(P("grp", "sub"), P("sub", "grp")),
        check_vma=False,
    )
```

```python
import jax
import jax.numpy as jnp
from jax import lax
from jax.experimental import pallas as pl
from jax.experimental.pallas import tpu as pltpu
from jax.sharding import PartitionSpec as P

BLOCK = 256
NY, NZH, NX, NZL, NC = 8, 2, 4, 6, 2
NZ = NZH * NZL
MESH = pl.DeviceIdType.MESH
F32, BF16 = jnp.float32, jnp.bfloat16

UP = ((4, 1), (3, 1), (2, 1), (1, 1), (3, 0), (2, 0), (1, 0))
DOWN = ((3, 1), (2, 1), (1, 1), (4, 0), (3, 0), (2, 0), (1, 0))


def body(
    attn_hbm, go_hbm, wv_hbm, ws_hbm, ga_ref, gw_ref,
    attn_ref, wv_ref, ws_ref, go, attn_t, w_own, w_got, rs_send, rs_got, own_part, own_sum, z_send, z_got, tile, tiles,
    in_sem, go_sem, wz_sem, ag_sem, rs_sem, z_sem, ar_sem,
):
    grp, sub = lax.axis_index("grp"), lax.axis_index("sub")
    y, zh = grp // NZH, grp % NZH
    x, zl, core = sub // (NZL * NC), (sub // NC) % NZL, sub % NC
    z, xc = zh * NZL + zl, x * NC + core
    cols, half, small = wv_ref.shape[1], wv_ref.shape[0] // 2, wv_ref.shape[0] // 4

    def along_y(d):
        return (((y + d) % NY) * NZH + zh, sub)

    def along_z(d):
        other = (z + d) % NZ
        return (y * NZH + other // NZL, (x * NZL + other % NZL) * NC + core)

    def along_xc(d):
        other = (xc + d) % (NX * NC)
        return (grp, ((other // NC) * NZL + zl) * NC + other % NC)

    sent = []

    def send(src, dst, sems, to):
        copy = pltpu.make_async_remote_copy(
            src_ref=src, dst_ref=dst, send_sem=sems[0], recv_sem=sems[1],
            device_id=to, device_id_type=MESH,
        )
        copy.start()
        sent.append(copy)
        return copy

    inputs = [
        pltpu.make_async_copy(src, dst, in_sem.at[i])
        for i, (src, dst) in enumerate(((attn_hbm, attn_ref), (wv_hbm, wv_ref), (ws_hbm, ws_ref)))
    ]
    for copy in inputs:
        copy.start()
    loads = {}
    for h in (1, 0):
        for d in (4, 5, 3, 6, 2, 7, 1, 0):
            chunk = ((y + d) % NY) * NZH + (zh if h == 0 else 1 - zh)
            loads[d, h] = pltpu.make_async_copy(
                go_hbm.at[:, pl.ds(pl.multiple_of(chunk * cols, cols), cols)],
                go.at[d, h],
                go_sem.at[d, h],
            )
            loads[d, h].start()

    barrier = pltpu.get_barrier_semaphore()
    partners = [along_y(d) for d in (1, 7)] + [along_z(d) for d in range(1, NZ)]
    partners += [along_xc(d) for d in range(1, NX * NC)]
    for to in partners:
        pl.semaphore_signal(barrier, inc=1, device_id=to, device_id_type=MESH)

    inputs[0].wait()
    attn_t[...] = attn_ref[...].T
    pl.semaphore_wait(barrier, len(partners))
    opposite = along_z(NZL)

    def part(d, h):
        if (d, h) in loads:
            loads.pop((d, h)).wait()
        return jnp.dot(attn_t[...], go[d, h], preferred_element_type=F32)

    ways = ((0, 1, UP), (1, -1, DOWN))
    got = {}

    def reduce_step(i):
        for way, sign, items in ways:
            d, h = items[i]
            own_part[way] = part((sign * d) % NY, h)
        for r in range(4):
            for way, sign, items in ways:
                d, h = items[i]
                piece = own_part[way, pl.ds(r * small, small)]
                if (way, d + 1, h, r) in got:
                    before, place = got[way, d + 1, h, r]
                    before.wait_recv()
                    piece = piece + rs_got[way, place].astype(F32)
                k = 4 * i + r
                rs_send[way, k] = piece.astype(BF16)
                copy = send(
                    rs_send.at[way, k], rs_got.at[way, k],
                    (rs_sem.at[0, way, k], rs_sem.at[1, way, k]), along_y(sign),
                )
                got[way, d, h, r] = (copy, k)

    def reduce_end(h):
        own_sum[h] = part(0, h)
        for r in range(4):
            for way, _, _ in ways:
                copy, k = got[way, 1, h, r]
                copy.wait_recv()
                own_sum[h, pl.ds(r * small, small)] += rs_got[way, k].astype(F32)

    def pass_on(src, way, sign, d, h, q):
        return send(
            src, w_got.at[way, d - 1, h, pl.ds(q * half, half)],
            (ag_sem.at[0, way, d - 1, h, q], ag_sem.at[1, way, d - 1, h, q]), along_y(sign),
        )

    gathered = {}

    def first_pass(h):
        for way, sign, _ in ways:
            for q in (0, 1):
                gathered[way, 1, h, q] = pass_on(w_own.at[h, pl.ds(q * half, half)], way, sign, 1, h, q)

    reduce_step(0)
    for copy in inputs[1:]:
        copy.wait()
    for j in range(cols // BLOCK):
        scale = jnp.broadcast_to(ws_ref[j:j + 1, :], (ws_ref.shape[1], ws_ref.shape[1])).T
        for k in range(j * BLOCK, (j + 1) * BLOCK, scale.shape[1]):
            piece = slice(k, k + scale.shape[1])
            w_own[0, :, piece] = (wv_ref[:, piece].astype(F32) * scale).astype(BF16)
    w_z = send(w_own.at[0], w_own.at[1], (wz_sem.at[0], wz_sem.at[1]), opposite)
    for i in (1, 2, 3, 4):
        reduce_step(i)
    first_pass(0)
    reduce_end(1)
    z_send[...] = own_sum[1].astype(BF16)
    to_opposite = send(z_send, z_got, (z_sem.at[0], z_sem.at[1]), opposite)
    for i in (5, 6):
        reduce_step(i)

    w_z.wait_recv()
    first_pass(1)
    reduce_end(0)

    def product(d, h, w):
        return lax.dot_general(go[d % NY, h], w, (((1,), (1,)), ((), ())), preferred_element_type=F32)

    total = product(0, 0, w_own[0]) + product(0, 1, w_own[1])

    def ring_step(d, h, total):
        arrived = []
        for q in (0, 1):
            for way, sign, _ in ways:
                if (way, d, h, q) not in gathered:
                    continue
                gathered[way, d, h, q].wait_recv()
                if q:
                    arrived.append((way, sign))
                if d < 3 or (d == 3 and h == way):
                    src = w_got.at[way, d - 1, h, pl.ds(q * half, half)]
                    gathered[way, d + 1, h, q] = pass_on(src, way, sign, d + 1, h, q)
        for way, sign in arrived:
            total = total + product(-sign * d, h, w_got[way, d - 1, h])
        return total

    def spread(stage, first, count, along):
        copies = []
        for d in range(1, count):
            slot = first + d - 1
            copies.append(
                send(tile.at[stage], tiles.at[slot], (ar_sem.at[0, slot], ar_sem.at[1, slot]), along(d))
            )
        return copies

    def collect(stage, first, copies):
        value = tile[stage]
        for d, copy in enumerate(copies):
            copy.wait_recv()
            value = value + tiles[first + d]
        return value

    total = ring_step(1, 0, total)
    to_opposite.wait_recv()
    summed = own_sum[0] + z_got[...].astype(F32)
    own_sum[0] = summed
    squares = jnp.sum((summed * summed).reshape(-1, 8, cols), axis=0)
    tile[0] = sum(squares[:, j * 128:(j + 1) * 128] for j in range(cols // 128))
    copies = spread(0, 0, NX * NC, along_xc)
    total = ring_step(1, 1, total)
    tile[1] = collect(0, 0, copies)
    copies = spread(1, NX * NC - 1, NZ, along_z)
    total = ring_step(2, 0, total)
    total = ring_step(2, 1, total)
    tile[2] = collect(1, NX * NC - 1, copies)
    copies = spread(2, NX * NC + NZ - 2, NY, along_y)
    total = ring_step(3, 0, total)
    total = ring_step(3, 1, total)
    squares = jnp.sum(collect(2, NX * NC + NZ - 2, copies), keepdims=True)
    count = NY * NZH * NX * NZL * NC * own_sum.shape[1] * cols
    clip = jnp.minimum(1.0, 0.5 * jnp.sqrt(jnp.full((1, 1), count, F32)) / jnp.sqrt(squares))
    gw_ref[...] = (own_sum[0] * clip).astype(BF16)
    total = ring_step(4, 0, total)
    total = ring_step(4, 1, total)
    ga_ref[...] = total.astype(BF16)
    for copy in sent:
        copy.wait_send()


def on_device(attn, grad_out, w_values, w_scales):
    tokens, head = attn.shape
    rows, cols = w_values.shape
    vmem = pl.BlockSpec(memory_space=pltpu.VMEM)
    dma = pltpu.SemaphoreType.DMA
    n_tiles = NY + NZ + NX * NC - 3
    return pl.pallas_call(
        body,
        out_shape=(
            jax.ShapeDtypeStruct((tokens, head), BF16),
            jax.ShapeDtypeStruct((rows, cols), BF16),
        ),
        in_specs=[pl.BlockSpec(memory_space=pltpu.HBM)] * 4,
        out_specs=(vmem, vmem),
        scratch_shapes=[
            pltpu.VMEM((tokens, head), BF16),
            pltpu.VMEM((rows, cols), BF16),
            pltpu.VMEM((cols // BLOCK, rows), F32),
            pltpu.VMEM((NY, 2, tokens, cols), BF16),
            pltpu.VMEM((head, tokens), BF16),
            pltpu.VMEM((2, rows, cols), BF16),
            pltpu.VMEM((2, 4, 2, rows, cols), BF16),
            pltpu.VMEM((2, 28, rows // 4, cols), BF16),
            pltpu.VMEM((2, 28, rows // 4, cols), BF16),
            pltpu.VMEM((2, rows, cols), F32),
            pltpu.VMEM((2, rows, cols), F32),
            pltpu.VMEM((rows, cols), BF16),
            pltpu.VMEM((rows, cols), BF16),
            pltpu.VMEM((3, 8, 128), F32),
            pltpu.VMEM((n_tiles, 8, 128), F32),
            dma((3,)),
            dma((NY, 2)),
            dma((2,)),
            dma((2, 2, 4, 2, 2)),
            dma((2, 2, 28)),
            dma((2,)),
            dma((2, n_tiles)),
        ],
        compiler_params=pltpu.CompilerParams(
            collective_id=0, has_side_effects=True, vmem_limit_bytes=40 * 2**20
        ),
        cost_estimate=pl.CostEstimate(
            flops=4 * tokens * head * 16 * cols, bytes_accessed=8 * 2**20, transcendentals=0
        ),
    )(*(pltpu.with_memory_space_constraint(a, pltpu.HBM) for a in (attn, grad_out, w_values, w_scales.T)))


def solution(mesh):
    placed = (P("grp", "sub"), P("grp", None), P("sub", "grp"), P("sub", "grp"))
    return jax.shard_map(
        on_device,
        mesh=mesh,
        in_specs=placed,
        out_specs=(P("grp", "sub"), P("sub", "grp")),
        check_vma=False,
    )
```
